32 devices in a mesh: blk: 8 (over z, core), fsdp: 4 (over y, x).
Axes of the slice: x: 2, y: 2, z: 4, core: 2. Of those that a mesh axis runs over, the one named last changes fastest.
Arguments:
- context: bfloat16 [8, 512, 2048], P('blk', 'fsdp'), may hold values from -6 to 6
- hidden: bfloat16 [8, 512, 4096], P('blk', 'fsdp'), may hold values from -6 to 6
- cotangent: bfloat16 [8, 512, 4096], P('blk', 'fsdp'), may hold values from -6 to 6
- gain: float32 [8, 4096], P('blk'), may hold values from 0.3 to 3
- weight: bfloat16 [8, 2048, 4096], P('blk', None, 'fsdp'), may hold values from -6 to 6
- step_counts: int32 [8], P('blk'), may hold values from 1 to 256
Outputs:
- new_weight: bfloat16 [8, 2048, 4096], P('blk', None, 'fsdp')
The draws below stay inside these ranges and needn't reach their ends.
All inputs are finite; a program needn't handle non-finite values.
Results may differ from the reference program's by a relative error of at most 0.0038.
Values may be sent and summed in bfloat16 or wider, within the bound.
A program may use at most 64 MiB of HBM per device.

```python
import math
import jax
import jax.numpy as jnp
from jax import lax

D = 4096
K = 2048
REPLICAS = 8
TOK_REP = 512


def with_ends(entries, rng, low, largest):
    longest = entries.shape.index(max(entries.shape))
    spots = []
    for shift in (0, 1):
        where = [jax.random.randint(jax.random.fold_in(rng, axis), (), 0, length) for axis, length in enumerate(entries.shape)]
        where[longest] = (where[longest] + shift) % entries.shape[longest]
        spots.append(tuple(where))
    return entries.at[spots[0]].set(low).at[spots[1]].set(largest)


def level_of(stream_key, extent, shards, smallest, top_value):
    def one(position, blocks):
        steps = jax.random.uniform(jax.random.fold_in(jax.random.fold_in(stream_key, 6), position), (blocks,), jnp.float32, smallest / len(shards), top_value / len(shards))
        return jnp.repeat(jnp.exp(steps), extent[position] // blocks).reshape((-1,) + (1,) * (len(extent) - position - 1))

    loudness = one(*shards[0])
    for cut in shards[1:]:
        loudness = loudness * one(*cut)
    return loudness


def centred(own_key, extent, spread, bound, cuts=(), kind=jnp.bfloat16):
    values = spread * jax.random.normal(own_key, extent, jnp.float32)
    if cuts:
        values = values * level_of(own_key, extent, cuts, -0.22, 0.18)
    return jnp.clip(values, -bound, bound).astype(kind)


def setup_inputs(seed: int = 0) -> dict:
    seeds = jax.random.split(jax.random.key(seed), 7)
    context = centred(seeds[0], (REPLICAS, TOK_REP, K), 1.0, 6.0, ((0, 8), (1, 4)))
    hidden = centred(seeds[1], (REPLICAS, TOK_REP, D), 1.0, 6.0, ((0, 8), (1, 4)))
    cotangent = centred(seeds[2], (REPLICAS, TOK_REP, D), 1.0, 6.0, ((0, 8), (1, 4)))
    gain = jnp.clip(jnp.exp(math.log(3.0) - 2.3025851 * jax.random.uniform(seeds[3], (REPLICAS, D), jnp.float32) ** level_of(seeds[3], (REPLICAS, D), ((0, 8),), -0.2, 0.2)), 0.3, 3.0)
    weight = centred(seeds[4], (REPLICAS, K, D), 1.0, 6.0, ((0, 8), (2, 4)))
    step_counts = with_ends(jax.random.randint(seeds[5], (REPLICAS,), 1, 257), jax.random.fold_in(seeds[5], 1), 1, 256).astype(jnp.int32)
    return dict(context=context, hidden=hidden, cotangent=cotangent, gain=gain, weight=weight, step_counts=step_counts)


def reference(context, hidden, cotangent, gain, weight, step_counts):
    scale = 1.0 / math.sqrt(K)
    rate = 0.5 * math.sqrt(K / TOK_REP)
    counts = step_counts.astype(jnp.float32)

    def one_replica(index):
        lower = (index + REPLICAS - 1) % REPLICAS
        upper = (index + 1) % REPLICAS
        inputs = context[index]
        own = weight[index]
        branch = (jnp.dot(inputs, own, preferred_element_type=jnp.float32) * scale).astype(jnp.bfloat16)
        residual_out = hidden[index].astype(jnp.float32) + branch.astype(jnp.float32)
        inv_rms = lax.rsqrt(lax.optimization_barrier(jnp.mean(residual_out * residual_out, axis=-1, keepdims=True)) + 1e-05)
        scaled = gain[index][None, :] * cotangent[index].astype(jnp.float32)
        cross = lax.optimization_barrier(jnp.mean(scaled * residual_out, axis=-1, keepdims=True))
        out_grad = (inv_rms * scaled - residual_out * inv_rms ** 3 * cross).astype(jnp.bfloat16)
        grad = jnp.dot(inputs.T, out_grad, preferred_element_type=jnp.float32) * scale
        low_count = counts[lower]
        own_count = counts[index]
        high_count = counts[upper]
        total = low_count + own_count + high_count
        mixed = (low_count * weight[lower].astype(jnp.float32) + own_count * own.astype(jnp.float32) + high_count * weight[upper].astype(jnp.float32)) / total
        return (mixed - rate * grad).astype(jnp.bfloat16)
    return lax.map(one_replica, jnp.arange(REPLICAS, dtype=jnp.int32))
```

```python
import functools
import math

import jax
import jax.numpy as jnp
from jax import lax
from jax.experimental import pallas as pl
from jax.experimental.pallas import tpu as pltpu
from jax.sharding import PartitionSpec as P

MESH = pl.DeviceIdType.MESH
CHUNKS = 16
DEPTH = 256
ROWS = 16
COLS = 256


def kernel(
    blocks,
    group,
    context,
    hidden,
    cotangent,
    gain,
    weight,
    count,
    out,
    low,
    high,
    own,
    acc,
    stage,
    tokens,
    branch_out,
    branch_in,
    grad_out,
    grad_in,
    hid,
    cot,
    gains,
    counts,
    w_send,
    w_recv,
    x_send,
    x_recv,
    b_send,
    b_recv,
    g_send,
    g_recv,
    c_send,
    c_recv,
    l_sem,
    o_sem,
):
    rank = lax.axis_index("blk")
    me = lax.axis_index("fsdp")
    up = lax.rem(rank + 1, blocks)
    down = lax.rem(rank + blocks - 1, blocks)
    per, width = context.shape
    part = weight.shape[1]
    model = part * group
    scale = 1.0 / math.sqrt(width)
    rate = 0.5 * math.sqrt(width / (per * group))
    piece = width // CHUNKS

    def peer(i):
        return lax.rem(me + i, group)

    def rows_of(p):
        return pl.ds(pl.multiple_of(p * per, per), per)

    barrier = pltpu.get_barrier_semaphore()
    for other in (up, down):
        pl.semaphore_signal(barrier, inc=1, device_id=(other, me), device_id_type=MESH)
    for i in range(1, group):
        pl.semaphore_signal(barrier, inc=1, device_id=(rank, peer(i)), device_id_type=MESH)
    pl.semaphore_wait(barrier, group + 1)

    def weight_copy(way, c):
        rows = pl.ds(c * piece, piece)
        other, landing = ((up, low), (down, high))[way]
        return pltpu.make_async_remote_copy(
            src_ref=weight.at[rows],
            dst_ref=landing.at[rows],
            send_sem=w_send.at[way, c],
            recv_sem=w_recv.at[way, c],
            device_id=(other, me),
            device_id_type=MESH,
        )

    def token_copy(source, slot, target):
        return pltpu.make_async_remote_copy(
            src_ref=source,
            dst_ref=tokens.at[rows_of(slot)],
            send_sem=x_send.at[target],
            recv_sem=x_recv.at[slot],
            device_id=(rank, target),
            device_id_type=MESH,
        )

    def branch_copy(slot, target):
        return pltpu.make_async_remote_copy(
            src_ref=branch_out.at[rows_of(target)],
            dst_ref=branch_in.at[rows_of(slot)],
            send_sem=b_send.at[target],
            recv_sem=b_recv.at[slot],
            device_id=(rank, target),
            device_id_type=MESH,
        )

    def grad_copy(slot, target):
        return pltpu.make_async_remote_copy(
            src_ref=grad_out.at[rows_of(target)],
            dst_ref=grad_in.at[rows_of(slot)],
            send_sem=g_send.at[target],
            recv_sem=g_recv.at[slot],
            device_id=(rank, target),
            device_id_type=MESH,
        )

    def count_copy(way):
        other = (up, down)[way]
        return pltpu.make_async_remote_copy(
            src_ref=counts.at[0],
            dst_ref=counts.at[1 + way],
            send_sem=c_send.at[way],
            recv_sem=c_recv.at[way],
            device_id=(other, me),
            device_id_type=MESH,
        )

    for c in range(CHUNKS):
        for way in range(2):
            weight_copy(way, c).start()
    for i in range(1, group):
        token_copy(context, me, peer(i)).start()

    loads = [
        pltpu.make_async_copy(context, tokens.at[rows_of(me)], l_sem.at[0]),
        pltpu.make_async_copy(weight, own, l_sem.at[1]),
        pltpu.make_async_copy(hidden, hid, l_sem.at[2]),
        pltpu.make_async_copy(cotangent, cot, l_sem.at[3]),
        pltpu.make_async_copy(gain, gains, l_sem.at[4]),
    ]
    for load in loads:
        load.start()

    counts[0] = jnp.full(counts.shape[1:], count[0], jnp.int32)
    for way in range(2):
        count_copy(way).start()

    loads[0].wait()
    loads[1].wait()

    def make_branch(p, target):
        block = tokens[rows_of(p)]

        @pl.loop(0, part // COLS)
        def _(n):
            columns = pl.ds(pl.multiple_of(n * COLS, COLS), COLS)
            dot = jnp.dot(block, own[:, columns], preferred_element_type=jnp.float32)
            target[rows_of(p), columns] = (dot * scale).astype(jnp.bfloat16)

    make_branch(me, branch_in)
    for i in range(1, group):
        p = peer(i)
        token_copy(context, p, p).wait_recv()
        make_branch(p, branch_out)
        branch_copy(me, p).start()

    for load in loads[2:]:
        load.wait()
    for i in range(1, group):
        p = peer(i)
        branch_copy(p, p).wait_recv()

    @pl.loop(0, per // ROWS)
    def _(t):
        rows = pl.ds(pl.multiple_of(t * ROWS, ROWS), ROWS)

        def terms(s):
            columns = pl.ds(s * part, part)
            slot = pl.ds(pl.multiple_of(s * per + t * ROWS, ROWS), ROWS)
            residual = hid[rows, columns].astype(jnp.float32) + branch_in[slot, :].astype(
                jnp.float32
            )
            scaled = gains[:, columns] * cot[rows, columns].astype(jnp.float32)
            return slot, residual, scaled

        squares = jnp.zeros((ROWS, 1), jnp.float32)
        cross = jnp.zeros((ROWS, 1), jnp.float32)
        for s in range(group):
            _, residual, scaled = terms(s)
            squares += jnp.sum(residual * residual, axis=-1, keepdims=True)
            cross += jnp.sum(scaled * residual, axis=-1, keepdims=True)
        inv_rms = lax.rsqrt(squares / model + 1e-05)
        factor = inv_rms * inv_rms * inv_rms * (cross / model)
        for s in range(group):
            slot, residual, scaled = terms(s)
            grad_out[slot, :] = (inv_rms * scaled - residual * factor).astype(jnp.bfloat16)

    for i in range(1, group):
        grad_copy(me, peer(i)).start()
    mine = pltpu.make_async_copy(grad_out.at[rows_of(me)], grad_in.at[rows_of(me)], l_sem.at[5])
    mine.start()

    for way in range(2):
        count_copy(way).wait_recv()
    own_c = counts[0][0:1, 0:1].astype(jnp.float32)
    low_c = counts[1][0:1, 0:1].astype(jnp.float32)
    high_c = counts[2][0:1, 0:1].astype(jnp.float32)
    total = low_c + own_c + high_c
    own_c, low_c, high_c = own_c / total, low_c / total, high_c / total

    mine.wait()
    for i in range(1, group):
        p = peer(i)
        grad_copy(p, p).wait_recv()

    @pl.loop(0, width // DEPTH)
    def _(k):
        rows = pl.ds(pl.multiple_of(k * DEPTH, DEPTH), DEPTH)
        grad = lax.dot_general(
            tokens[:, rows],
            grad_in[...],
            (((0,), (0,)), ((), ())),
            preferred_element_type=jnp.float32,
        )
        acc[rows, :] = own_c * own[rows, :].astype(jnp.float32) - (rate * scale) * grad

    def result(c):
        rows = pl.ds(c * piece, piece)
        return pltpu.make_async_copy(stage.at[rows], out.at[rows], o_sem.at[c])

    for c in range(CHUNKS):
        rows = pl.ds(c * piece, piece)
        for way in range(2):
            weight_copy(way, c).wait_recv()
        stage[rows, :] = (
            acc[rows, :]
            + low_c * low[rows, :].astype(jnp.float32)
            + high_c * high[rows, :].astype(jnp.float32)
        ).astype(jnp.bfloat16)
        result(c).start()

    for i in range(1, group):
        p = peer(i)
        token_copy(context, me, p).wait_send()
        branch_copy(me, p).wait_send()
        grad_copy(me, p).wait_send()
    for way in range(2):
        count_copy(way).wait_send()
        for c in range(CHUNKS):
            weight_copy(way, c).wait_send()
    for c in range(CHUNKS):
        result(c).wait()


def body(context, hidden, cotangent, gain, weight, step_counts):
    blocks = lax.axis_size("blk")
    group = lax.axis_size("fsdp")
    _, per, width = context.shape
    part = weight.shape[2]
    half = jnp.bfloat16
    flops = 4 * per * group * width * part
    hbm = pl.BlockSpec(memory_space=pl.ANY)
    new = pl.pallas_call(
        functools.partial(kernel, blocks, group),
        out_shape=jax.ShapeDtypeStruct((width, part), half),
        in_specs=[hbm] * 5 + [pl.BlockSpec(memory_space=pltpu.SMEM)],
        out_specs=hbm,
        scratch_shapes=[
            pltpu.VMEM((width, part), half),
            pltpu.VMEM((width, part), half),
            pltpu.VMEM((width, part), half),
            pltpu.VMEM((width, part), jnp.float32),
            pltpu.VMEM((width, part), half),
            pltpu.VMEM((per * group, width), half),
            pltpu.VMEM((per * group, part), half),
            pltpu.VMEM((per * group, part), half),
            pltpu.VMEM((per * group, part), half),
            pltpu.VMEM((per * group, part), half),
            pltpu.VMEM((per, part * group), half),
            pltpu.VMEM((per, part * group), half),
            pltpu.VMEM((1, part * group), jnp.float32),
            pltpu.VMEM((3, 8, 128), jnp.int32),
            pltpu.SemaphoreType.DMA((2, CHUNKS)),
            pltpu.SemaphoreType.DMA((2, CHUNKS)),
            pltpu.SemaphoreType.DMA((group,)),
            pltpu.SemaphoreType.DMA((group,)),
            pltpu.SemaphoreType.DMA((group,)),
            pltpu.SemaphoreType.DMA((group,)),
            pltpu.SemaphoreType.DMA((group,)),
            pltpu.SemaphoreType.DMA((group,)),
            pltpu.SemaphoreType.DMA((2,)),
            pltpu.SemaphoreType.DMA((2,)),
            pltpu.SemaphoreType.DMA((6,)),
            pltpu.SemaphoreType.DMA((CHUNKS,)),
        ],
        compiler_params=pltpu.CompilerParams(
            collective_id=1, has_side_effects=True, vmem_limit_bytes=54 * 2**20
        ),
        cost_estimate=pl.CostEstimate(
            flops=flops, bytes_accessed=24 * 2**20, transcendentals=0
        ),
    )(context[0], hidden[0], cotangent[0], gain, weight[0], step_counts)
    return new[None]


def solution(mesh):
    return jax.shard_map(
        body,
        mesh=mesh,
        in_specs=(
            P("blk", "fsdp", None),
            P("blk", "fsdp", None),
            P("blk", "fsdp", None),
            P("blk", None),
            P("blk", None, "fsdp"),
            P("blk"),
        ),
        out_specs=P("blk", None, "fsdp"),
        check_vma=False,
    )
```

```python
import functools
import math

import jax
import jax.numpy as jnp
from jax import lax
from jax.experimental import pallas as pl
from jax.experimental.pallas import tpu as pltpu
from jax.sharding import PartitionSpec as P

MESH = pl.DeviceIdType.MESH
CHUNKS = 16
DEPTH = 256
ROWS = 16
COLS = 256


def kernel(
    blocks,
    group,
    context,
    hidden,
    cotangent,
    gain,
    weight,
    count,
    out,
    low,
    high,
    own,
    acc,
    stage,
    tokens,
    branch_out,
    branch_in,
    grad_out,
    grad_in,
    hid,
    cot,
    gains,
    counts,
    w_send,
    w_recv,
    x_send,
    x_recv,
    b_send,
    b_recv,
    g_send,
    g_recv,
    c_send,
    c_recv,
    l_sem,
    o_sem,
):
    rank = lax.axis_index("blk")
    me = lax.axis_index("fsdp")
    up = lax.rem(rank + 1, blocks)
    down = lax.rem(rank + blocks - 1, blocks)
    per, width = context.shape
    part = weight.shape[1]
    model = part * group
    scale = 1.0 / math.sqrt(width)
    rate = 0.5 * math.sqrt(width / (per * group))
    piece = width // CHUNKS

    def peer(i):
        return lax.rem(me + i, group)

    def rows_of(p):
        return pl.ds(pl.multiple_of(p * per, per), per)

    barrier = pltpu.get_barrier_semaphore()
    for other in (up, down):
        pl.semaphore_signal(barrier, inc=1, device_id=(other, me), device_id_type=MESH)
    for i in range(1, group):
        pl.semaphore_signal(barrier, inc=1, device_id=(rank, peer(i)), device_id_type=MESH)
    pl.semaphore_wait(barrier, group + 1)

    def weight_copy(way, c):
        rows = pl.ds(c * piece, piece)
        other, landing = ((up, low), (down, high))[way]
        return pltpu.make_async_remote_copy(
            src_ref=weight.at[rows],
            dst_ref=landing.at[rows],
            send_sem=w_send.at[way, c],
            recv_sem=w_recv.at[way, c],
            device_id=(other, me),
            device_id_type=MESH,
        )

    def token_copy(source, slot, target):
        return pltpu.make_async_remote_copy(
            src_ref=source,
            dst_ref=tokens.at[rows_of(slot)],
            send_sem=x_send.at[target],
            recv_sem=x_recv.at[slot],
            device_id=(rank, target),
            device_id_type=MESH,
        )

    def branch_copy(slot, target):
        return pltpu.make_async_remote_copy(
            src_ref=branch_out.at[rows_of(target)],
            dst_ref=branch_in.at[rows_of(slot)],
            send_sem=b_send.at[target],
            recv_sem=b_recv.at[slot],
            device_id=(rank, target),
            device_id_type=MESH,
        )

    def grad_copy(slot, target):
        return pltpu.make_async_remote_copy(
            src_ref=grad_out.at[rows_of(target)],
            dst_ref=grad_in.at[rows_of(slot)],
            send_sem=g_send.at[target],
            recv_sem=g_recv.at[slot],
            device_id=(rank, target),
            device_id_type=MESH,
        )

    def count_copy(way):
        other = (up, down)[way]
        return pltpu.make_async_remote_copy(
            src_ref=counts.at[0],
            dst_ref=counts.at[1 + way],
            send_sem=c_send.at[way],
            recv_sem=c_recv.at[way],
            device_id=(other, me),
            device_id_type=MESH,
        )

    counts[0] = jnp.full(counts.shape[1:], count[0], jnp.int32)
    for way in range(2):
        count_copy(way).start()

    for c in range(CHUNKS):
        for way in range(2):
            weight_copy(way, c).start()
    for i in range(1, group):
        token_copy(context, me, peer(i)).start()

    loads = [
        pltpu.make_async_copy(context, tokens.at[rows_of(me)], l_sem.at[0]),
        pltpu.make_async_copy(weight, own, l_sem.at[1]),
        pltpu.make_async_copy(hidden, hid, l_sem.at[2]),
        pltpu.make_async_copy(cotangent, cot, l_sem.at[3]),
        pltpu.make_async_copy(gain, gains, l_sem.at[4]),
    ]
    for load in loads:
        load.start()

    loads[0].wait()
    loads[1].wait()

    def make_branch(p, target):
        block = tokens[rows_of(p)]

        @pl.loop(0, part // COLS)
        def _(n):
            columns = pl.ds(pl.multiple_of(n * COLS, COLS), COLS)
            dot = jnp.dot(block, own[:, columns], preferred_element_type=jnp.float32)
            target[rows_of(p), columns] = (dot * scale).astype(jnp.bfloat16)

    make_branch(me, branch_in)
    for i in range(1, group):
        p = peer(i)
        token_copy(context, p, p).wait_recv()
        make_branch(p, branch_out)
        branch_copy(me, p).start()

    for load in loads[2:]:
        load.wait()
    for i in range(1, group):
        p = peer(i)
        branch_copy(p, p).wait_recv()

    @pl.loop(0, per // ROWS)
    def _(t):
        rows = pl.ds(pl.multiple_of(t * ROWS, ROWS), ROWS)

        def terms(s):
            columns = pl.ds(s * part, part)
            slot = pl.ds(pl.multiple_of(s * per + t * ROWS, ROWS), ROWS)
            residual = hid[rows, columns].astype(jnp.float32) + branch_in[slot, :].astype(
                jnp.float32
            )
            scaled = gains[:, columns] * cot[rows, columns].astype(jnp.float32)
            return slot, residual, scaled

        squares = jnp.zeros((ROWS, 1), jnp.float32)
        cross = jnp.zeros((ROWS, 1), jnp.float32)
        for s in range(group):
            _, residual, scaled = terms(s)
            squares += jnp.sum(residual * residual, axis=-1, keepdims=True)
            cross += jnp.sum(scaled * residual, axis=-1, keepdims=True)
        inv_rms = lax.rsqrt(squares / model + 1e-05)
        factor = inv_rms * inv_rms * inv_rms * (cross / model)
        for s in range(group):
            slot, residual, scaled = terms(s)
            grad_out[slot, :] = (inv_rms * scaled - residual * factor).astype(jnp.bfloat16)

    for i in range(1, group):
        grad_copy(me, peer(i)).start()
    mine = pltpu.make_async_copy(grad_out.at[rows_of(me)], grad_in.at[rows_of(me)], l_sem.at[5])
    mine.start()

    for way in range(2):
        count_copy(way).wait_recv()
    own_c = counts[0][0:1, 0:1].astype(jnp.float32)
    low_c = counts[1][0:1, 0:1].astype(jnp.float32)
    high_c = counts[2][0:1, 0:1].astype(jnp.float32)
    total = low_c + own_c + high_c
    own_c, low_c, high_c = own_c / total, low_c / total, high_c / total

    mine.wait()
    for i in range(1, group):
        p = peer(i)
        grad_copy(p, p).wait_recv()

    @pl.loop(0, width // DEPTH)
    def _(k):
        rows = pl.ds(pl.multiple_of(k * DEPTH, DEPTH), DEPTH)
        grad = lax.dot_general(
            tokens[:, rows],
            grad_in[...],
            (((0,), (0,)), ((), ())),
            preferred_element_type=jnp.float32,
        )
        acc[rows, :] = own_c * own[rows, :].astype(jnp.float32) - (rate * scale) * grad

    def result(c):
        rows = pl.ds(c * piece, piece)
        return pltpu.make_async_copy(stage.at[rows], out.at[rows], o_sem.at[c])

    for c in range(CHUNKS):
        rows = pl.ds(c * piece, piece)
        for way in range(2):
            weight_copy(way, c).wait_recv()
        stage[rows, :] = (
            acc[rows, :]
            + low_c * low[rows, :].astype(jnp.float32)
            + high_c * high[rows, :].astype(jnp.float32)
        ).astype(jnp.bfloat16)
        result(c).start()

    for i in range(1, group):
        p = peer(i)
        token_copy(context, me, p).wait_send()
        branch_copy(me, p).wait_send()
        grad_copy(me, p).wait_send()
    for way in range(2):
        count_copy(way).wait_send()
        for c in range(CHUNKS):
            weight_copy(way, c).wait_send()
    for c in range(CHUNKS):
        result(c).wait()


def body(context, hidden, cotangent, gain, weight, step_counts):
    blocks = lax.axis_size("blk")
    group = lax.axis_size("fsdp")
    _, per, width = context.shape
    part = weight.shape[2]
    half = jnp.bfloat16
    flops = 4 * per * group * width * part
    hbm = pl.BlockSpec(memory_space=pltpu.HBM)
    new = pl.pallas_call(
        functools.partial(kernel, blocks, group),
        out_shape=jax.ShapeDtypeStruct((width, part), half),
        in_specs=[hbm] * 5 + [pl.BlockSpec(memory_space=pltpu.SMEM)],
        out_specs=pl.BlockSpec(memory_space=pl.ANY),
        scratch_shapes=[
            pltpu.VMEM((width, part), half),
            pltpu.VMEM((width, part), half),
            pltpu.VMEM((width, part), half),
            pltpu.VMEM((width, part), jnp.float32),
            pltpu.VMEM((width, part), half),
            pltpu.VMEM((per * group, width), half),
            pltpu.VMEM((per * group, part), half),
            pltpu.VMEM((per * group, part), half),
            pltpu.VMEM((per * group, part), half),
            pltpu.VMEM((per * group, part), half),
            pltpu.VMEM((per, part * group), half),
            pltpu.VMEM((per, part * group), half),
            pltpu.VMEM((1, part * group), jnp.float32),
            pltpu.VMEM((3, 8, 128), jnp.int32),
            pltpu.SemaphoreType.DMA((2, CHUNKS)),
            pltpu.SemaphoreType.DMA((2, CHUNKS)),
            pltpu.SemaphoreType.DMA((group,)),
            pltpu.SemaphoreType.DMA((group,)),
            pltpu.SemaphoreType.DMA((group,)),
            pltpu.SemaphoreType.DMA((group,)),
            pltpu.SemaphoreType.DMA((group,)),
            pltpu.SemaphoreType.DMA((group,)),
            pltpu.SemaphoreType.DMA((2,)),
            pltpu.SemaphoreType.DMA((2,)),
            pltpu.SemaphoreType.DMA((6,)),
            pltpu.SemaphoreType.DMA((CHUNKS,)),
        ],
        compiler_params=pltpu.CompilerParams(
            collective_id=1, has_side_effects=True, vmem_limit_bytes=46 * 2**20
        ),
        cost_estimate=pl.CostEstimate(
            flops=flops, bytes_accessed=24 * 2**20, transcendentals=0
        ),
    )(
        *(
            pltpu.with_memory_space_constraint(x, pltpu.HBM)
            for x in (context[0], hidden[0], cotangent[0], gain, weight[0])
        ),
        step_counts,
    )
    return new[None]


def solution(mesh):
    return jax.shard_map(
        body,
        mesh=mesh,
        in_specs=(
            P("blk", "fsdp", None),
            P("blk", "fsdp", None),
            P("blk", "fsdp", None),
            P("blk", None),
            P("blk", None, "fsdp"),
            P("blk"),
        ),
        out_specs=P("blk", None, "fsdp"),
        check_vma=False,
    )
```

```python
import functools
import math

import jax
import jax.numpy as jnp
from jax import lax
from jax.experimental import pallas as pl
from jax.experimental.pallas import tpu as pltpu
from jax.sharding import PartitionSpec as P

MESH = pl.DeviceIdType.MESH
CUTS = (0, 8, 16, 24, 32, 40, 48, 56, 60, 62, 64)
CHUNKS = len(CUTS) - 1
DEPTH = 256
ROWS = 16
COLS = 256


def kernel(
    blocks,
    group,
    context,
    hidden,
    cotangent,
    gain,
    weight,
    count,
    out,
    low,
    high,
    own,
    acc,
    tokens,
    branch_out,
    branch_in,
    grad_out,
    grad_in,
    hid,
    cot,
    gains,
    counts,
    w_send,
    w_recv,
    x_send,
    x_recv,
    b_send,
    b_recv,
    g_send,
    g_recv,
    c_send,
    c_recv,
    l_sem,
):
    rank = lax.axis_index("blk")
    me = lax.axis_index("fsdp")
    up = lax.rem(rank + 1, blocks)
    down = lax.rem(rank + blocks - 1, blocks)
    per, width = context.shape
    part = weight.shape[1]
    model = part * group
    scale = 1.0 / math.sqrt(width)
    rate = 0.5 * math.sqrt(width / (per * group))
    step = width // CUTS[-1]

    def peer(i):
        return lax.rem(me + i, group)

    def rows_of(p):
        return pl.ds(pl.multiple_of(p * per, per), per)

    barrier = pltpu.get_barrier_semaphore()
    for other in (up, down):
        pl.semaphore_signal(barrier, inc=1, device_id=(other, me), device_id_type=MESH)
    for i in range(1, group):
        pl.semaphore_signal(barrier, inc=1, device_id=(rank, peer(i)), device_id_type=MESH)
    pl.semaphore_wait(barrier, group + 1)

    def weight_copy(way, c):
        rows = pl.ds(CUTS[c] * step, (CUTS[c + 1] - CUTS[c]) * step)
        other, landing = ((up, low), (down, high))[way]
        return pltpu.make_async_remote_copy(
            src_ref=weight.at[rows],
            dst_ref=landing.at[rows],
            send_sem=w_send.at[way, c],
            recv_sem=w_recv.at[way, c],
            device_id=(other, me),
            device_id_type=MESH,
        )

    def token_copy(source, slot, target):
        return pltpu.make_async_remote_copy(
            src_ref=source,
            dst_ref=tokens.at[rows_of(slot)],
            send_sem=x_send.at[target],
            recv_sem=x_recv.at[slot],
            device_id=(rank, target),
            device_id_type=MESH,
        )

    def branch_copy(slot, target):
        return pltpu.make_async_remote_copy(
            src_ref=branch_out.at[rows_of(target)],
            dst_ref=branch_in.at[rows_of(slot)],
            send_sem=b_send.at[target],
            recv_sem=b_recv.at[slot],
            device_id=(rank, target),
            device_id_type=MESH,
        )

    def grad_copy(slot, target):
        return pltpu.make_async_remote_copy(
            src_ref=grad_out.at[rows_of(target)],
            dst_ref=grad_in.at[rows_of(slot)],
            send_sem=g_send.at[target],
            recv_sem=g_recv.at[slot],
            device_id=(rank, target),
            device_id_type=MESH,
        )

    def count_copy(way):
        other = (up, down)[way]
        return pltpu.make_async_remote_copy(
            src_ref=counts.at[0],
            dst_ref=counts.at[1 + way],
            send_sem=c_send.at[way],
            recv_sem=c_recv.at[way],
            device_id=(other, me),
            device_id_type=MESH,
        )

    counts[0] = jnp.full(counts.shape[1:], count[0], jnp.int32)
    for way in range(2):
        count_copy(way).start()

    for c in range(CHUNKS):
        for way in range(2):
            weight_copy(way, c).start()
    for i in range(1, group):
        token_copy(context, me, peer(i)).start()

    loads = [
        pltpu.make_async_copy(context, tokens.at[rows_of(me)], l_sem.at[0]),
        pltpu.make_async_copy(weight, own, l_sem.at[1]),
        pltpu.make_async_copy(hidden, hid, l_sem.at[2]),
        pltpu.make_async_copy(cotangent, cot, l_sem.at[3]),
        pltpu.make_async_copy(gain, gains, l_sem.at[4]),
    ]
    for load in loads:
        load.start()

    loads[0].wait()
    loads[1].wait()

    def make_branch(p, target):
        block = tokens[rows_of(p)]

        @pl.loop(0, part // COLS)
        def _(n):
            columns = pl.ds(pl.multiple_of(n * COLS, COLS), COLS)
            dot = jnp.dot(block, own[:, columns], preferred_element_type=jnp.float32)
            target[rows_of(p), columns] = (dot * scale).astype(jnp.bfloat16)

    make_branch(me, branch_in)
    for i in range(1, group):
        p = peer(i)
        token_copy(context, p, p).wait_recv()
        make_branch(p, branch_out)
        branch_copy(me, p).start()

    for load in loads[2:]:
        load.wait()
    for i in range(1, group):
        p = peer(i)
        branch_copy(p, p).wait_recv()

    @pl.loop(0, per // ROWS)
    def _(t):
        rows = pl.ds(pl.multiple_of(t * ROWS, ROWS), ROWS)

        def terms(s):
            columns = pl.ds(s * part, part)
            slot = pl.ds(pl.multiple_of(s * per + t * ROWS, ROWS), ROWS)
            residual = hid[rows, columns].astype(jnp.float32) + branch_in[slot, :].astype(
                jnp.float32
            )
            scaled = gains[:, columns] * cot[rows, columns].astype(jnp.float32)
            return slot, residual, scaled

        squares = jnp.zeros((ROWS, 1), jnp.float32)
        cross = jnp.zeros((ROWS, 1), jnp.float32)
        for s in range(group):
            _, residual, scaled = terms(s)
            squares += jnp.sum(residual * residual, axis=-1, keepdims=True)
            cross += jnp.sum(scaled * residual, axis=-1, keepdims=True)
        inv_rms = lax.rsqrt(squares / model + 1e-05)
        factor = inv_rms * inv_rms * inv_rms * (cross / model)
        for s in range(group):
            slot, residual, scaled = terms(s)
            grad_out[slot, :] = (inv_rms * scaled - residual * factor).astype(jnp.bfloat16)

    for i in range(1, group):
        grad_copy(me, peer(i)).start()
    mine = pltpu.make_async_copy(grad_out.at[rows_of(me)], grad_in.at[rows_of(me)], l_sem.at[5])
    mine.start()

    for way in range(2):
        count_copy(way).wait_recv()
    own_c = counts[0][0:1, 0:1].astype(jnp.float32)
    low_c = counts[1][0:1, 0:1].astype(jnp.float32)
    high_c = counts[2][0:1, 0:1].astype(jnp.float32)
    total = low_c + own_c + high_c
    own_c, low_c, high_c = own_c / total, low_c / total, high_c / total

    mine.wait()
    for i in range(1, group):
        p = peer(i)
        grad_copy(p, p).wait_recv()

    @pl.loop(0, width // DEPTH)
    def _(k):
        rows = pl.ds(pl.multiple_of(k * DEPTH, DEPTH), DEPTH)
        grad = lax.dot_general(
            tokens[:, rows],
            grad_in[...],
            (((0,), (0,)), ((), ())),
            preferred_element_type=jnp.float32,
        )
        acc[rows, :] = own_c * own[rows, :].astype(jnp.float32) - (rate * scale) * grad

    for i in range(1, group):
        p = peer(i)
        token_copy(context, me, p).wait_send()
        branch_copy(me, p).wait_send()
        grad_copy(me, p).wait_send()
    for way in range(2):
        count_copy(way).wait_send()

    for c in range(CHUNKS):
        rows = pl.ds(CUTS[c] * step, (CUTS[c + 1] - CUTS[c]) * step)
        for way in range(2):
            weight_copy(way, c).wait_recv()
        out[rows, :] = (
            acc[rows, :]
            + low_c * low[rows, :].astype(jnp.float32)
            + high_c * high[rows, :].astype(jnp.float32)
        ).astype(jnp.bfloat16)

    for way in range(2):
        for c in range(CHUNKS):
            weight_copy(way, c).wait_send()


def body(context, hidden, cotangent, gain, weight, step_counts):
    blocks = lax.axis_size("blk")
    group = lax.axis_size("fsdp")
    _, per, width = context.shape
    part = weight.shape[2]
    half = jnp.bfloat16
    flops = 4 * per * group * width * part
    hbm = pl.BlockSpec(memory_space=pltpu.HBM)
    new = pl.pallas_call(
        functools.partial(kernel, blocks, group),
        out_shape=jax.ShapeDtypeStruct((width, part), half),
        in_specs=[hbm] * 5 + [pl.BlockSpec(memory_space=pltpu.SMEM)],
        out_specs=pl.BlockSpec(memory_space=pltpu.VMEM),
        scratch_shapes=[
            pltpu.VMEM((width, part), half),
            pltpu.VMEM((width, part), half),
            pltpu.VMEM((width, part), half),
            pltpu.VMEM((width, part), jnp.float32),
            pltpu.VMEM((per * group, width), half),
            pltpu.VMEM((per * group, part), half),
            pltpu.VMEM((per * group, part), half),
            pltpu.VMEM((per * group, part), half),
            pltpu.VMEM((per * group, part), half),
            pltpu.VMEM((per, part * group), half),
            pltpu.VMEM((per, part * group), half),
            pltpu.VMEM((1, part * group), jnp.float32),
            pltpu.VMEM((3, 8, 128), jnp.int32),
            pltpu.SemaphoreType.DMA((2, CHUNKS)),
            pltpu.SemaphoreType.DMA((2, CHUNKS)),
            pltpu.SemaphoreType.DMA((group,)),
            pltpu.SemaphoreType.DMA((group,)),
            pltpu.SemaphoreType.DMA((group,)),
            pltpu.SemaphoreType.DMA((group,)),
            pltpu.SemaphoreType.DMA((group,)),
            pltpu.SemaphoreType.DMA((group,)),
            pltpu.SemaphoreType.DMA((2,)),
            pltpu.SemaphoreType.DMA((2,)),
            pltpu.SemaphoreType.DMA((6,)),
        ],
        compiler_params=pltpu.CompilerParams(
            collective_id=1, has_side_effects=True, vmem_limit_bytes=46 * 2**20
        ),
        cost_estimate=pl.CostEstimate(
            flops=flops, bytes_accessed=24 * 2**20, transcendentals=0
        ),
    )(
        *(
            pltpu.with_memory_space_constraint(x, pltpu.HBM)
            for x in (context[0], hidden[0], cotangent[0], gain, weight[0])
        ),
        step_counts,
    )
    return new[None]


def solution(mesh):
    return jax.shard_map(
        body,
        mesh=mesh,
        in_specs=(
            P("blk", "fsdp", None),
            P("blk", "fsdp", None),
            P("blk", "fsdp", None),
            P("blk", None),
            P("blk", None, "fsdp"),
            P("blk"),
        ),
        out_specs=P("blk", None, "fsdp"),
        check_vma=False,
    )
```
